32 devices in a mesh: slides: 2 (over y), rows: 4 (over z), cols: 2 (over x), chan: 2 (over core).
Axes of the slice: x: 2, y: 2, z: 4, core: 2. Of those that a mesh axis runs over, the one named last changes fastest.
Arguments:
- features: bfloat16 [128, 64, 384], P(('slides', 'rows'), 'cols', 'chan'), parts along dimension 0, may hold values from -6 to 6
- gate_input: bfloat16 [128, 64, 384], P(('slides', 'rows'), 'cols', 'chan'), parts along dimension 0, may hold values from -6 to 6
- decay_idx: int32 [128, 64], P(('slides', 'rows'), 'cols'), parts along dimension 0, may hold values from 0 to 15
- log_table: float32 [16, 384], P(None, 'chan'), may hold values from -1 to 0, as said below
- state_rate: float32 [16], replicated, may hold values from 0.5 to 2
- proj_row: bfloat16 [384, 32], P('chan'), may hold values from -0.0390625 to 0.0390625
- proj_col: bfloat16 [384, 32], P('chan'), may hold values from -0.0390625 to 0.0390625
- conv_w: float32 [3, 3, 384], P(None, None, 'chan'), may hold values from -0.5 to 0.5
- conv_b: float32 [384], P('chan'), may hold values from -0.5 to 0.5
- d_skip: float32 [384], P('chan'), may hold values from 0.5 to 1.5
Outputs:
- output: bfloat16 [128, 64, 384], P(('slides', 'rows'), 'cols', 'chan'), parts along dimension 0
The draws below stay inside these ranges and needn't reach their ends.
There are 2 independent parts, one for each index of `slides`. The reference program is written for one: setup_inputs(seed, part) draws one part's arguments, and reference() takes and returns one part's arrays. A program takes and returns all parts, laid end to end along the dimension named above; an argument that names none is the same for every part. Nothing has to cross between parts.
Inputs may be any that keep to these rules, and one draw needn't show every extreme that they name: `log_table`: every entry is negative.
All inputs are finite; a program needn't handle non-finite values.
Results may differ from the reference program's by a relative error of at most 0.0061.
Values may be sent and summed in bfloat16 or wider, within the bound.
A program may use at most 128 MiB of HBM per device.

```python
import math
import jax
import jax.numpy as jnp
from jax import lax

INNER_WIDTH = 384
S = 16
K = 16
PATCH_ROWS = 64
PATCH_COLUMNS = 64


def draw_log_table(key, part):
    key_mask = jax.random.fold_in(key, 11)
    key_slow = jax.random.fold_in(key, 12)
    key_quick = jax.random.fold_in(key, 13)
    key_factor = jax.random.fold_in(key, 14)
    spike_key = jax.random.fold_in(key, 15)
    share = 0.5
    quick_mask = jax.random.uniform(key_mask, (INNER_WIDTH,), jnp.float32) < share
    slow_rate = jnp.exp(jax.random.uniform(key_slow, (INNER_WIDTH,), jnp.float32, minval=jnp.log(0.1 / PATCH_ROWS), maxval=jnp.log(1.0 / PATCH_ROWS)))
    quick_rate = jnp.exp(jax.random.uniform(key_quick, (INNER_WIDTH,), jnp.float32, minval=jnp.log(1.0 / 50.0), maxval=jnp.log(1.0 / 30.0)))
    baseline_rate = jnp.where(quick_mask, quick_rate, slow_rate)
    factors = jnp.exp(jax.random.uniform(key_factor, (K - 1, INNER_WIDTH), jnp.float32, minval=jnp.log(0.5), maxval=jnp.log(2.0)))
    spike_penalty = -jnp.log(jax.random.uniform(spike_key, (INNER_WIDTH,), jnp.float32, minval=0.5, maxval=0.8))
    leading_row = baseline_rate + spike_penalty
    table = jnp.concatenate([leading_row[None, :], baseline_rate[None, :] * factors], axis=0)
    return (-table).astype(jnp.float32)


def draw_decay_idx(key, part):
    key_levels = jax.random.fold_in(key, 21)
    spike_key = jax.random.fold_in(key, 22)
    level_values = jax.random.randint(key_levels, (PATCH_ROWS, PATCH_COLUMNS), 1, K)
    spike_sample = jax.random.randint(spike_key, (PATCH_ROWS, PATCH_COLUMNS), 0, 256)
    return jnp.where(spike_sample == 0, 0, level_values).astype(jnp.int32)


def levels(stream_key, extent, shards, least, largest):
    def one(axis_at, shards_of):
        heights = jax.random.uniform(jax.random.fold_in(jax.random.fold_in(stream_key, 6), axis_at), (shards_of,), jnp.float32, least / len(shards), largest / len(shards))
        return jnp.repeat(jnp.exp(heights), extent[axis_at] // shards_of).reshape((-1,) + (1,) * (len(extent) - axis_at - 1))

    level = one(*shards[0])
    for cut in shards[1:]:
        level = level * one(*cut)
    return level


def gaussian(own_key, dims, deviation, limit, shards=(), held_as=jnp.bfloat16):
    loudness = levels(own_key, dims, shards, -0.22, 0.18) if shards else 1.0
    array = jax.random.normal(own_key, dims, jnp.float32) * deviation * loudness
    return jnp.minimum(jnp.maximum(array, -limit), limit).astype(held_as)


def setup_inputs(seed: int = 0, part: int = 0) -> dict:
    seeds = jax.random.split(jax.random.key(seed), 11)
    own_keys = jax.random.split(jax.random.fold_in(seeds[10], part), 11)
    return {
        "features": gaussian(own_keys[0], (PATCH_ROWS, PATCH_COLUMNS, INNER_WIDTH), 1.0, 6.0, ((0, 4), (1, 2), (2, 2))),
        "gate_input": gaussian(own_keys[1], (PATCH_ROWS, PATCH_COLUMNS, INNER_WIDTH), 1.0, 6.0, ((0, 4), (1, 2), (2, 2))),
        "decay_idx": draw_decay_idx(jax.random.fold_in(jax.random.fold_in(seeds[10], part), 71), part),
        "log_table": draw_log_table(jax.random.fold_in(seeds[10], 71), part),
        "state_rate": jnp.clip(jnp.exp(jax.random.uniform(seeds[4], (S,), jnp.float32, math.log(0.5), math.log(2.0))), 0.5, 2.0),
        "proj_row": gaussian(seeds[5], (INNER_WIDTH, 2 * S), (64 * INNER_WIDTH) ** -0.5, 0.0390625, ((0, 2),)),
        "proj_col": gaussian(seeds[6], (INNER_WIDTH, 2 * S), (64 * INNER_WIDTH) ** -0.5, 0.0390625, ((0, 2),)),
        "conv_w": jnp.clip(jax.random.uniform(seeds[7], (3, 3, INNER_WIDTH), jnp.float32, -0.5, 0.5) * levels(seeds[7], (3, 3, INNER_WIDTH), ((2, 2),), -0.4, 0.0), -0.5, 0.5),
        "conv_b": jnp.clip(jax.random.uniform(seeds[8], (INNER_WIDTH,), jnp.float32, -0.5, 0.5) * levels(seeds[8], (INNER_WIDTH,), ((0, 2),), -0.4, 0.0), -0.5, 0.5),
        "d_skip": jnp.clip(0.5 + 1.0 * jax.random.uniform(seeds[9], (INNER_WIDTH,), jnp.float32) ** levels(seeds[9], (INNER_WIDTH,), ((0, 2),), -0.2, 0.2), 0.5, 1.5),
    }


def combine_pair(earlier, latter):
    return earlier[0] + latter[0], latter[1] + jnp.exp(latter[0]) * earlier[1]


def axis_scan(values, log_decays, coeffs, state_rate):
    num_states = state_rate.shape[0]

    def one_state(summed, which_state):
        state_scale = state_rate[which_state]
        drive_col = lax.dynamic_index_in_dim(coeffs, which_state, 2, keepdims=True)
        out_col = lax.dynamic_index_in_dim(coeffs, which_state + num_states, 2, keepdims=True)
        cumulative, states = lax.associative_scan(combine_pair, (log_decays * state_scale, drive_col * values), axis=0)
        return summed + out_col * states, None

    summed, unused = lax.scan(one_state, jnp.zeros(values.shape, jnp.float32), jnp.arange(num_states, dtype=jnp.int32))
    return summed


def reference(features, gate_input, decay_idx, log_table, state_rate, proj_row, proj_col, conv_w, conv_b, d_skip):
    log_decays = jnp.take(log_table, decay_idx, axis=0)
    feats_wide = features.astype(jnp.float32)
    coeff_row = jnp.dot(features, proj_row, preferred_element_type=jnp.float32)
    swept_rows = axis_scan(feats_wide.transpose(1, 0, 2), log_decays.transpose(1, 0, 2), coeff_row.transpose(1, 0, 2), state_rate).transpose(1, 0, 2)
    row_out = (swept_rows + d_skip * feats_wide).astype(jnp.bfloat16)
    padded = jnp.pad(row_out.astype(jnp.float32), ((1, 1), (1, 1), (0, 0)))
    convolved = jnp.zeros(feats_wide.shape, jnp.float32) + conv_b
    for offset_row in range(3):
        for offset_col in range(3):
            convolved = convolved + conv_w[offset_row, offset_col] * padded[offset_row:offset_row + PATCH_ROWS, offset_col:offset_col + PATCH_COLUMNS]
    middle = jax.nn.silu(convolved).astype(jnp.bfloat16)
    middle_wide = middle.astype(jnp.float32)
    coeff_col = jnp.dot(middle, proj_col, preferred_element_type=jnp.float32)
    combined = axis_scan(middle_wide, log_decays, coeff_col, state_rate) + d_skip * middle_wide
    return (combined * jax.nn.silu(gate_input.astype(jnp.float32))).astype(jnp.bfloat16)
```

```python
import functools
import math

import jax
import jax.numpy as jnp
from jax import lax
from jax.experimental import pallas as pl
from jax.experimental.pallas import tpu as pltpu
from jax.sharding import PartitionSpec as P

MESH = pl.DeviceIdType.MESH
LANES = 128
GROUP = 8
PAD = 8
F32 = jnp.float32
BF16 = jnp.bfloat16
SIDES = ((-1, 0), (1, 0), (0, -1), (0, 1), (-1, -1), (-1, 1), (1, -1), (1, 1))


def opposite(side):
    return SIDES.index((-side[0], -side[1]))


def layer(
    dims,
    feats_ref,
    gate_ref,
    idx_ref,
    table_ref,
    rate_ref,
    proj_row_ref,
    proj_col_ref,
    conv_w_ref,
    conv_b_ref,
    skip_ref,
    out_ref,
    xf,
    lf,
    hot,
    cf,
    csend,
    crecv,
    ro,
    par,
    mb,
    rsend,
    rrecv,
    zsend,
    zrecv,
    edge_rows,
    edge_cols,
    got_rows,
    got_cols,
    coeff_sems,
    row_sems,
    col_sems,
    edge_sems,
):
    H, W, E, S, K, nz, nx = dims
    NT = -(-E // LANES)
    WP = W + 2 * PAD
    widths = [min(LANES, E - LANES * t) for t in range(NT)]
    z, x, c, sl = (lax.axis_index(a) for a in ("rows", "cols", "chan", "slides"))
    sibling = (sl, z, x, 1 - c)

    def exists(side):
        dz, dx = side
        parts = []
        if dz:
            parts.append(z > 0 if dz < 0 else z < nz - 1)
        if dx:
            parts.append(x > 0 if dx < 0 else x < nx - 1)
        return functools.reduce(jnp.logical_and, parts)

    def device(side):
        return (sl, z + side[0], x + side[1], c)

    barrier = pltpu.get_barrier_semaphore()
    pl.semaphore_signal(barrier, inc=1, device_id=sibling, device_id_type=MESH)
    for side in SIDES:

        @pl.when(exists(side))
        def _(side=side):
            pl.semaphore_signal(barrier, inc=1, device_id=device(side), device_id_type=MESH)

    flat = feats_ref[...].reshape(H * W, E)
    csend[0] = jnp.dot(flat, proj_row_ref[...], preferred_element_type=F32)
    peers_z = jnp.where(z > 0, 1, 0) + jnp.where(z < nz - 1, 1, 0)
    peers_x = jnp.where(x > 0, 1, 0) + jnp.where(x < nx - 1, 1, 0)
    pl.semaphore_wait(barrier, 1 + peers_z + peers_x + peers_z * peers_x)

    def coeff_copy(n):
        return pltpu.make_async_remote_copy(
            src_ref=csend.at[n],
            dst_ref=crecv.at[n],
            send_sem=coeff_sems.at[0, n],
            recv_sem=coeff_sems.at[1, n],
            device_id=sibling,
            device_id_type=MESH,
        )

    coeff_copy(0).start()

    for t in range(NT):
        w_t = widths[t]
        lo = t * LANES
        if w_t < LANES:
            xf[t] = jnp.zeros((H * W, LANES), F32)
            lf[t] = jnp.zeros((H * W, LANES), F32)
            par[t] = jnp.zeros((16, LANES), F32)
        xf[t, :, 0:w_t] = flat[:, lo : lo + w_t].astype(F32)
        for a in range(3):
            par[t, 3 * a : 3 * a + 3, 0:w_t] = conv_w_ref[a, :, lo : lo + w_t]
        par[t, 9:10, 0:w_t] = conv_b_ref[:, lo : lo + w_t]
        par[t, 10:11, 0:w_t] = skip_ref[:, lo : lo + w_t]
        ro[t] = jnp.zeros(((H + 2) * WP, LANES), F32)
    idx_t = idx_ref[...].astype(F32).T
    entry = lax.rem(lax.broadcasted_iota(jnp.int32, (W, 3 * K), 1), K).astype(F32)
    for h in range(H):
        hot[h * W : (h + 1) * W, :] = jnp.where(idx_t[:, h : h + 1] == entry, 1.0, 0.0)
    table = table_ref[...] * math.log2(math.e)
    first = table.astype(BF16)
    rest = table - first.astype(F32)
    second = rest.astype(BF16)
    third = (rest - second.astype(F32)).astype(BF16)
    logs = jnp.dot(
        hot[...].astype(BF16),
        jnp.concatenate([first, second, third], axis=0),
        preferred_element_type=F32,
    )
    for t in range(NT):
        lf[t, :, 0 : widths[t]] = logs[:, t * LANES : t * LANES + widths[t]]
    skips = [par[t, 10:11, :] for t in range(NT)]

    coeff_copy(0).wait()
    cf[:, 0 : 2 * S] = csend[0] + crecv[0]

    def scan_step(rows_at, states):
        coeffs = cf[rows_at, :]
        vals = [xf[t, rows_at, :] for t in range(NT)]
        logs_at = [lf[t, rows_at, :] for t in range(NT)]
        sums = [vals[t] * skips[t] for t in range(NT)]
        new = []
        for s in range(S):
            b = jnp.broadcast_to(coeffs[:, s : s + 1], (GROUP, LANES))
            o = jnp.broadcast_to(coeffs[:, S + s : S + s + 1], (GROUP, LANES))
            for t in range(NT):
                state = jnp.exp2(logs_at[t] * rate_ref[s]) * states[s * NT + t] + b * vals[t]
                sums[t] = sums[t] + o * state
                new.append(state)
        return sums, tuple(new)

    def carry_copy(send, recv, sems, n, side):
        return pltpu.make_async_remote_copy(
            src_ref=send.at[n],
            dst_ref=recv.at[n],
            send_sem=sems.at[0, n],
            recv_sem=sems.at[1, n],
            device_id=device(side),
            device_id_type=MESH,
        )

    def load_carry(recv, n):
        states = []
        for s in range(0, S, 2):
            pair = [recv[n, t, s * GROUP : (s + 2) * GROUP, :].astype(F32) for t in range(NT)]
            states += [p[:GROUP] for p in pair] + [p[GROUP:] for p in pair]
        return tuple(states)

    def store_carry(send, n, states):
        for t in range(NT):
            for s in range(0, S, 2):
                pair = jnp.concatenate([states[s * NT + t], states[(s + 1) * NT + t]], axis=0)
                send[n, t, s * GROUP : (s + 2) * GROUP, :] = pair.astype(BF16)

    @pl.when(x == 0)
    def _():
        rrecv[...] = jnp.zeros(rrecv.shape, BF16)

    for n in range(H // GROUP):

        @pl.when(x > 0)
        def _():
            carry_copy(rsend, rrecv, row_sems, n, (0, 1)).wait_recv()

        def row_step(w, states):
            sums, new = scan_step(pl.ds(n * GROUP * W + w, GROUP, stride=W), states)
            for t in range(NT):
                ro[t, pl.ds((n * GROUP + 1) * WP + PAD + w, GROUP, stride=WP), :] = (
                    sums[t].astype(BF16).astype(F32)
                )
            return new

        ends = lax.fori_loop(0, W, row_step, load_carry(rrecv, n))

        @pl.when(x < nx - 1)
        def _():
            store_carry(rsend, n, ends)
            carry_copy(rsend, rrecv, row_sems, n, (0, 1)).start()

    for t in range(NT):
        for n, h in enumerate((0, H - 1)):
            at = (h + 1) * WP + PAD
            edge_rows[n, t] = ro[t, at : at + W, :].astype(BF16)
        for n, w in enumerate((0, W - 1)):
            edge_cols[n, t] = ro[t, pl.ds(WP + PAD + w, H, stride=WP), :].astype(BF16)

    def edge_copy(k):
        dz, dx = SIDES[k]
        if dx == 0:
            src, dst = edge_rows.at[(dz + 1) // 2], got_rows.at[(1 - dz) // 2]
        else:
            src = edge_cols.at[(dx + 1) // 2]
            dst = got_cols.at[opposite(SIDES[k]) - 2]
        return pltpu.make_async_remote_copy(
            src_ref=src,
            dst_ref=dst,
            send_sem=edge_sems.at[0, k],
            recv_sem=edge_sems.at[1, opposite(SIDES[k])],
            device_id=device(SIDES[k]),
            device_id_type=MESH,
        )

    def edge_arrival(k):
        dz, dx = SIDES[k]
        buf = got_rows.at[(dz + 1) // 2] if dx == 0 else got_cols.at[k - 2]
        src = edge_rows.at[0] if dx == 0 else edge_cols.at[0]
        return pltpu.make_async_remote_copy(
            src_ref=src,
            dst_ref=buf,
            send_sem=edge_sems.at[0, k],
            recv_sem=edge_sems.at[1, k],
            device_id=device(SIDES[k]),
            device_id_type=MESH,
        )

    for k, side in enumerate(SIDES):

        @pl.when(exists(side))
        def _(k=k):
            edge_copy(k).start()

    for k, side in enumerate(SIDES):

        @pl.when(exists(side))
        def _(k=k, side=side):
            edge_arrival(k).wait_recv()
            dz, dx = side
            row = {-1: 0, 0: 1, 1: H + 1}[dz]
            col = {-1: PAD - 1, 0: PAD, 1: PAD + W}[dx]
            for t in range(NT):
                if dx == 0:
                    ro[t, row * WP + col : row * WP + col + W, :] = got_rows[
                        (dz + 1) // 2, t
                    ].astype(F32)
                elif dz == 0:
                    ro[t, pl.ds(row * WP + col, H, stride=WP), :] = got_cols[k - 2, t].astype(F32)
                else:
                    pick = H - 1 if dz < 0 else 0
                    ro[t, row * WP + col : row * WP + col + 1, :] = got_cols[k - 2, t].astype(F32)[
                        pick : pick + 1
                    ]

    def conv_step(h, unused):
        for t in range(NT):
            acc = jnp.broadcast_to(par[t, 9:10, :], (W, LANES))
            for a in range(3):
                for b in range(3):
                    start = (h + a) * WP
                    acc = acc + par[t, 3 * a + b : 3 * a + b + 1, :] * ro[
                        t, pl.ds(start + PAD - 1 + b, W), :
                    ]
            mid = (acc / (1.0 + jnp.exp(-acc))).astype(BF16)
            at = pl.ds(pl.multiple_of(h * W, W), W)
            xf[t, at, :] = mid.astype(F32)
            mb[at, t * LANES : t * LANES + widths[t]] = mid[:, 0 : widths[t]]
        return unused

    lax.fori_loop(0, H, conv_step, 0)

    csend[1] = jnp.dot(mb[...], proj_col_ref[...], preferred_element_type=F32)
    coeff_copy(1).start()
    coeff_copy(1).wait()
    cf[:, 0 : 2 * S] = csend[1] + crecv[1]

    @pl.when(z == 0)
    def _():
        zrecv[...] = jnp.zeros(zrecv.shape, BF16)

    for n in range(W // GROUP):

        @pl.when(z > 0)
        def _():
            carry_copy(zsend, zrecv, col_sems, n, (1, 0)).wait_recv()

        def col_step(h, states):
            at = pl.ds(pl.multiple_of(h * W + n * GROUP, GROUP), GROUP)
            sums, new = scan_step(at, states)
            for t in range(NT):
                xf[t, at, :] = sums[t]
            return new

        ends = lax.fori_loop(0, H, col_step, load_carry(zrecv, n))

        @pl.when(z < nz - 1)
        def _():
            store_carry(zsend, n, ends)
            carry_copy(zsend, zrecv, col_sems, n, (1, 0)).start()

    def gate_step(h, unused):
        at = pl.ds(pl.multiple_of(h * W, W), W)
        for t in range(NT):
            g = gate_ref[h, :, t * LANES : t * LANES + widths[t]].astype(F32)
            v = xf[t, at, 0 : widths[t]] * g / (1.0 + jnp.exp(-g))
            out_ref[h, :, t * LANES : t * LANES + widths[t]] = v.astype(BF16)
        return unused

    lax.fori_loop(0, H, gate_step, 0)

    for k, side in enumerate(SIDES):

        @pl.when(exists(side))
        def _(k=k):
            edge_copy(k).wait_send()

    @pl.when(x < nx - 1)
    def _():
        for n in range(H // GROUP):
            carry_copy(rsend, rrecv, row_sems, n, (0, 1)).wait_send()

    @pl.when(z < nz - 1)
    def _():
        for n in range(W // GROUP):
            carry_copy(zsend, zrecv, col_sems, n, (1, 0)).wait_send()


def shards(
    nz,
    nx,
    features,
    gate_input,
    decay_idx,
    log_table,
    state_rate,
    proj_row,
    proj_col,
    conv_w,
    conv_b,
    d_skip,
):
    H, W, E = features.shape
    S, K = state_rate.shape[0], log_table.shape[0]
    NT = -(-E // LANES)
    WP = W + 2 * PAD
    vmem = pl.BlockSpec(memory_space=pltpu.VMEM)
    smem = pl.BlockSpec(memory_space=pltpu.SMEM)
    dma = pltpu.SemaphoreType.DMA
    return pl.pallas_call(
        functools.partial(layer, (H, W, E, S, K, nz, nx)),
        out_shape=jax.ShapeDtypeStruct((H, W, E), BF16),
        in_specs=[vmem] * 4 + [smem] + [vmem] * 5,
        out_specs=vmem,
        scratch_shapes=[
            pltpu.VMEM((NT, H * W, LANES), F32),
            pltpu.VMEM((NT, H * W, LANES), F32),
            pltpu.VMEM((H * W, 3 * K), F32),
            pltpu.VMEM((H * W, LANES), F32),
            pltpu.VMEM((2, H * W, 2 * S), F32),
            pltpu.VMEM((2, H * W, 2 * S), F32),
            pltpu.VMEM((NT, (H + 2) * WP, LANES), F32),
            pltpu.VMEM((NT, 16, LANES), F32),
            pltpu.VMEM((H * W, E), BF16),
            pltpu.VMEM((H // GROUP, NT, S * GROUP, LANES), BF16),
            pltpu.VMEM((H // GROUP, NT, S * GROUP, LANES), BF16),
            pltpu.VMEM((W // GROUP, NT, S * GROUP, LANES), BF16),
            pltpu.VMEM((W // GROUP, NT, S * GROUP, LANES), BF16),
            pltpu.VMEM((2, NT, W, LANES), BF16),
            pltpu.VMEM((2, NT, H, LANES), BF16),
            pltpu.VMEM((2, NT, W, LANES), BF16),
            pltpu.VMEM((6, NT, H, LANES), BF16),
            dma((2, 2)),
            dma((2, H // GROUP)),
            dma((2, W // GROUP)),
            dma((2, 8)),
        ],
        compiler_params=pltpu.CompilerParams(
            collective_id=0, has_side_effects=True, vmem_limit_bytes=40 * 1024 * 1024
        ),
    )(
        features,
        gate_input,
        decay_idx,
        log_table,
        state_rate,
        proj_row,
        proj_col,
        conv_w,
        conv_b.reshape(1, E),
        d_skip.reshape(1, E),
    )


def solution(mesh):
    tile = P(("slides", "rows"), "cols", "chan")
    placed = (
        tile,
        tile,
        P(("slides", "rows"), "cols"),
        P(None, "chan"),
        P(),
        P("chan", None),
        P("chan", None),
        P(None, None, "chan"),
        P("chan"),
        P("chan"),
    )
    return jax.shard_map(
        functools.partial(shards, mesh.shape["rows"], mesh.shape["cols"]),
        mesh=mesh,
        in_specs=placed,
        out_specs=tile,
        check_vma=False,
    )
```

```python
import functools
import math

import jax
import jax.numpy as jnp
from jax import lax
from jax.experimental import pallas as pl
from jax.experimental.pallas import tpu as pltpu
from jax.sharding import PartitionSpec as P

MESH = pl.DeviceIdType.MESH
LANES = 128
GROUP = 8
PAD = 8
SPLIT = 2
UNROLL = 16
F32 = jnp.float32
BF16 = jnp.bfloat16
SIDES = ((-1, 0), (1, 0), (0, -1), (0, 1), (-1, -1), (-1, 1), (1, -1), (1, 1))


def opposite(side):
    return SIDES.index((-side[0], -side[1]))


def project(vals, proj_t):
    return lax.dot_general(vals, proj_t, (((1,), (1,)), ((), ())), preferred_element_type=F32)


def layer(
    dims,
    feats_hbm,
    gate_hbm,
    idx_ref,
    table_ref,
    rate_ref,
    proj_row_ref,
    proj_col_ref,
    conv_w_ref,
    conv_b_ref,
    skip_ref,
    out_ref,
    feats_ref,
    gate_ref,
    xf,
    yf,
    lf,
    hot,
    cf,
    csend,
    crecv,
    ro,
    par,
    mb,
    rsend,
    rrecv,
    zsend,
    zrecv,
    edge_rows,
    edge_cols,
    got_rows,
    got_cols,
    coeff_sems,
    row_sems,
    col_sems,
    edge_sems,
    load_sems,
):
    H, W, E, S, K, nz, nx = dims
    NT = -(-E // LANES)
    WP = W + 2 * PAD
    widths = [min(LANES, E - LANES * t) for t in range(NT)]
    z, x, c, sl = (lax.axis_index(a) for a in ("rows", "cols", "chan", "slides"))
    sibling = (sl, z, x, 1 - c)

    def exists(side):
        dz, dx = side
        parts = []
        if dz:
            parts.append(z > 0 if dz < 0 else z < nz - 1)
        if dx:
            parts.append(x > 0 if dx < 0 else x < nx - 1)
        return functools.reduce(jnp.logical_and, parts)

    def device(side):
        return (sl, z + side[0], x + side[1], c)

    feats_load = pltpu.make_async_copy(feats_hbm, feats_ref, load_sems.at[0])
    gate_load = pltpu.make_async_copy(gate_hbm, gate_ref, load_sems.at[1])
    feats_load.start()
    gate_load.start()
    barrier = pltpu.get_barrier_semaphore()
    pl.semaphore_signal(barrier, inc=1, device_id=sibling, device_id_type=MESH)
    for side in SIDES:

        @pl.when(exists(side))
        def _(side=side):
            pl.semaphore_signal(barrier, inc=1, device_id=device(side), device_id_type=MESH)

    feats_load.wait()
    flat = feats_ref[...].reshape(H * W, E)
    csend[0] = project(flat, proj_row_ref[...])
    peers_z = jnp.where(z > 0, 1, 0) + jnp.where(z < nz - 1, 1, 0)
    peers_x = jnp.where(x > 0, 1, 0) + jnp.where(x < nx - 1, 1, 0)
    pl.semaphore_wait(barrier, 1 + peers_z + peers_x + peers_z * peers_x)

    def coeff_copy(n):
        return pltpu.make_async_remote_copy(
            src_ref=csend.at[n],
            dst_ref=crecv.at[n],
            send_sem=coeff_sems.at[0, n],
            recv_sem=coeff_sems.at[1, n],
            device_id=sibling,
            device_id_type=MESH,
        )

    coeff_copy(0).start()

    for t in range(NT):
        w_t = widths[t]
        lo = t * LANES
        if w_t < LANES:
            xf[t] = jnp.zeros((H * W, LANES), F32)
            lf[t] = jnp.zeros((H * W, LANES), F32)
            par[t] = jnp.zeros((16, LANES), F32)
        xf[t, :, 0:w_t] = flat[:, lo : lo + w_t].astype(F32)
        for a in range(3):
            par[t, 3 * a : 3 * a + 3, 0:w_t] = conv_w_ref[a, :, lo : lo + w_t]
        par[t, 9:10, 0:w_t] = conv_b_ref[:, lo : lo + w_t]
        par[t, 10:11, 0:w_t] = skip_ref[:, lo : lo + w_t]
        ro[t] = jnp.zeros(((H + 2) * WP, LANES), F32)
    idx_t = idx_ref[...].astype(F32).T
    entry = lax.rem(lax.broadcasted_iota(jnp.int32, (W, 3 * K), 1), K).astype(F32)
    for h in range(H):
        hot[h * W : (h + 1) * W, :] = jnp.where(idx_t[:, h : h + 1] == entry, 1.0, 0.0)
    table = table_ref[...] * math.log2(math.e)
    first = table.astype(BF16)
    rest = table - first.astype(F32)
    second = rest.astype(BF16)
    third = (rest - second.astype(F32)).astype(BF16)
    logs = jnp.dot(
        hot[...].astype(BF16),
        jnp.concatenate([first, second, third], axis=0),
        preferred_element_type=F32,
    )
    for t in range(NT):
        lf[t, :, 0 : widths[t]] = logs[:, t * LANES : t * LANES + widths[t]]
    skips = [par[t, 10:11, :] for t in range(NT)]

    coeff_copy(0).wait()
    cf[:, 0 : 2 * S] = csend[0] + crecv[0]

    SQ = S // SPLIT
    packed = widths[-1] <= LANES // 2
    low_lanes = lax.broadcasted_iota(jnp.int32, (GROUP, LANES), 1) < LANES // 2

    def scan_step(rows_at, q, sums, states):
        coeffs = cf[rows_at, :]
        vals = [xf[t, rows_at, :] for t in range(NT)]
        logs_at = [lf[t, rows_at, :] for t in range(NT)]
        if q == 0:
            sums = [vals[t] * skips[t] for t in range(NT)]
        new = []
        for k in range(SQ):
            s = q * SQ + k
            b = jnp.broadcast_to(coeffs[:, s : s + 1], (GROUP, LANES))
            o = jnp.broadcast_to(coeffs[:, S + s : S + s + 1], (GROUP, LANES))
            for t in range(NT):
                state = jnp.exp2(logs_at[t] * rate_ref[s]) * states[k * NT + t] + b * vals[t]
                sums[t] = sums[t] + o * state
                new.append(state)
        return sums, tuple(new)

    def carry_copy(send, recv, sems, n, side):
        return pltpu.make_async_remote_copy(
            src_ref=send.at[n],
            dst_ref=recv.at[n],
            send_sem=sems.at[0, n],
            recv_sem=sems.at[1, n],
            device_id=device(side),
            device_id_type=MESH,
        )

    def half_turn(v):
        return pltpu.roll(v, LANES // 2, axis=1)

    def load_carry(recv, n):
        states = [None] * (SQ * NT)
        at = 0
        for t in range(NT):
            tail = packed and t == NT - 1
            for k in range(0, SQ, 4 if tail else 2):
                pair = recv[n, at : at + 2 * GROUP, :].astype(F32)
                at += 2 * GROUP
                for i in range(2):
                    v = pair[i * GROUP : (i + 1) * GROUP]
                    if tail:
                        states[(k + 2 * i) * NT + t] = jnp.where(low_lanes, v, 0.0)
                        states[(k + 2 * i + 1) * NT + t] = jnp.where(low_lanes, half_turn(v), 0.0)
                    else:
                        states[(k + i) * NT + t] = v
        return tuple(states)

    def store_carry(send, n, states):
        at = 0
        for t in range(NT):
            tail = packed and t == NT - 1
            own = [states[k * NT + t] for k in range(SQ)]
            if tail:
                own = [own[k] + half_turn(own[k + 1]) for k in range(0, SQ, 2)]
            for k in range(0, len(own), 2):
                pair = jnp.concatenate([own[k], own[k + 1]], axis=0)
                send[n, at : at + 2 * GROUP, :] = pair.astype(BF16)
                at += 2 * GROUP

    @pl.when(x == 0)
    def _():
        rrecv[...] = jnp.zeros(rrecv.shape, BF16)

    for n in range(H // GROUP):
        for q in range(SPLIT):
            m = n * SPLIT + q

            @pl.when(x > 0)
            def _():
                carry_copy(rsend, rrecv, row_sems, m, (0, 1)).wait_recv()

            def row_step(w, states):
                to = pl.ds((n * GROUP + 1) * WP + PAD + w, GROUP, stride=WP)
                sums = [ro[t, to, :] for t in range(NT)] if q else None
                at = pl.ds(n * GROUP * W + w, GROUP, stride=W)
                sums, new = scan_step(at, q, sums, states)
                for t in range(NT):
                    last = q == SPLIT - 1
                    ro[t, to, :] = sums[t].astype(BF16).astype(F32) if last else sums[t]
                return new

            ends = lax.fori_loop(0, W, row_step, load_carry(rrecv, m), unroll=UNROLL)

            @pl.when(x < nx - 1)
            def _():
                store_carry(rsend, m, ends)
                carry_copy(rsend, rrecv, row_sems, m, (0, 1)).start()

    for t in range(NT):
        for n, h in enumerate((0, H - 1)):
            at = (h + 1) * WP + PAD
            edge_rows[n, t] = ro[t, at : at + W, :].astype(BF16)
        for n, w in enumerate((0, W - 1)):
            edge_cols[n, t] = ro[t, pl.ds(WP + PAD + w, H, stride=WP), :].astype(BF16)

    def edge_copy(k):
        dz, dx = SIDES[k]
        if dx == 0:
            src, dst = edge_rows.at[(dz + 1) // 2], got_rows.at[(1 - dz) // 2]
        else:
            src = edge_cols.at[(dx + 1) // 2]
            dst = got_cols.at[opposite(SIDES[k]) - 2]
        return pltpu.make_async_remote_copy(
            src_ref=src,
            dst_ref=dst,
            send_sem=edge_sems.at[0, k],
            recv_sem=edge_sems.at[1, opposite(SIDES[k])],
            device_id=device(SIDES[k]),
            device_id_type=MESH,
        )

    def edge_arrival(k):
        dz, dx = SIDES[k]
        buf = got_rows.at[(dz + 1) // 2] if dx == 0 else got_cols.at[k - 2]
        src = edge_rows.at[0] if dx == 0 else edge_cols.at[0]
        return pltpu.make_async_remote_copy(
            src_ref=src,
            dst_ref=buf,
            send_sem=edge_sems.at[0, k],
            recv_sem=edge_sems.at[1, k],
            device_id=device(SIDES[k]),
            device_id_type=MESH,
        )

    for k, side in enumerate(SIDES):

        @pl.when(exists(side))
        def _(k=k):
            edge_copy(k).start()

    for k, side in enumerate(SIDES):

        @pl.when(exists(side))
        def _(k=k, side=side):
            edge_arrival(k).wait_recv()
            dz, dx = side
            row = {-1: 0, 0: 1, 1: H + 1}[dz]
            col = {-1: PAD - 1, 0: PAD, 1: PAD + W}[dx]
            for t in range(NT):
                if dx == 0:
                    ro[t, row * WP + col : row * WP + col + W, :] = got_rows[
                        (dz + 1) // 2, t
                    ].astype(F32)
                elif dz == 0:
                    ro[t, pl.ds(row * WP + col, H, stride=WP), :] = got_cols[k - 2, t].astype(F32)
                else:
                    pick = H - 1 if dz < 0 else 0
                    ro[t, row * WP + col : row * WP + col + 1, :] = got_cols[k - 2, t].astype(F32)[
                        pick : pick + 1
                    ]

    def conv_step(h, unused):
        for t in range(NT):
            acc = jnp.broadcast_to(par[t, 9:10, :], (W, LANES))
            for a in range(3):
                for b in range(3):
                    start = (h + a) * WP
                    acc = acc + par[t, 3 * a + b : 3 * a + b + 1, :] * ro[
                        t, pl.ds(start + PAD - 1 + b, W), :
                    ]
            mid = (acc / (1.0 + jnp.exp(-acc))).astype(BF16)
            at = pl.ds(pl.multiple_of(h * W, W), W)
            xf[t, at, :] = mid.astype(F32)
            mb[at, t * LANES : t * LANES + widths[t]] = mid[:, 0 : widths[t]]
        return unused

    lax.fori_loop(0, H, conv_step, 0, unroll=4)

    csend[1] = project(mb[...], proj_col_ref[...])
    coeff_copy(1).start()
    coeff_copy(1).wait()
    cf[:, 0 : 2 * S] = csend[1] + crecv[1]

    @pl.when(z == 0)
    def _():
        zrecv[...] = jnp.zeros(zrecv.shape, BF16)

    for n in range(W // GROUP):
        for q in range(SPLIT):
            m = n * SPLIT + q

            @pl.when(z > 0)
            def _():
                carry_copy(zsend, zrecv, col_sems, m, (1, 0)).wait_recv()

            def col_step(h, states):
                at = pl.ds(pl.multiple_of(h * W + n * GROUP, GROUP), GROUP)
                sums = [yf[t, at, :] for t in range(NT)] if q else None
                sums, new = scan_step(at, q, sums, states)
                for t in range(NT):
                    yf[t, at, :] = sums[t]
                return new

            ends = lax.fori_loop(0, H, col_step, load_carry(zrecv, m), unroll=UNROLL)

            @pl.when(z < nz - 1)
            def _():
                store_carry(zsend, m, ends)
                carry_copy(zsend, zrecv, col_sems, m, (1, 0)).start()

    gate_load.wait()
    def gate_step(h, unused):
        at = pl.ds(pl.multiple_of(h * W, W), W)
        for t in range(NT):
            g = gate_ref[h, :, t * LANES : t * LANES + widths[t]].astype(F32)
            v = yf[t, at, 0 : widths[t]] * g / (1.0 + jnp.exp(-g))
            out_ref[h, :, t * LANES : t * LANES + widths[t]] = v.astype(BF16)
        return unused

    lax.fori_loop(0, H, gate_step, 0, unroll=4)

    for k, side in enumerate(SIDES):

        @pl.when(exists(side))
        def _(k=k):
            edge_copy(k).wait_send()

    @pl.when(x < nx - 1)
    def _():
        for n in range(H // GROUP * SPLIT):
            carry_copy(rsend, rrecv, row_sems, n, (0, 1)).wait_send()

    @pl.when(z < nz - 1)
    def _():
        for n in range(W // GROUP * SPLIT):
            carry_copy(zsend, zrecv, col_sems, n, (1, 0)).wait_send()


def shards(
    nz,
    nx,
    features,
    gate_input,
    decay_idx,
    log_table,
    state_rate,
    proj_row,
    proj_col,
    conv_w,
    conv_b,
    d_skip,
):
    H, W, E = features.shape
    S, K = state_rate.shape[0], log_table.shape[0]
    NT = -(-E // LANES)
    WP = W + 2 * PAD
    tail = E - (NT - 1) * LANES
    depth = (2 * NT - (tail <= LANES // 2)) * (S // SPLIT) * GROUP // 2
    vmem = pl.BlockSpec(memory_space=pltpu.VMEM)
    hbm = pl.BlockSpec(memory_space=pl.ANY)
    smem = pl.BlockSpec(memory_space=pltpu.SMEM)
    dma = pltpu.SemaphoreType.DMA
    return pl.pallas_call(
        functools.partial(layer, (H, W, E, S, K, nz, nx)),
        out_shape=jax.ShapeDtypeStruct((H, W, E), BF16),
        in_specs=[hbm] * 2 + [vmem] * 2 + [smem] + [vmem] * 5,
        out_specs=vmem,
        scratch_shapes=[
            pltpu.VMEM((H, W, E), BF16),
            pltpu.VMEM((H, W, E), BF16),
            pltpu.VMEM((NT, H * W, LANES), F32),
            pltpu.VMEM((NT, H * W, LANES), F32),
            pltpu.VMEM((NT, H * W, LANES), F32),
            pltpu.VMEM((H * W, 3 * K), F32),
            pltpu.VMEM((H * W, LANES), F32),
            pltpu.VMEM((2, H * W, 2 * S), F32),
            pltpu.VMEM((2, H * W, 2 * S), F32),
            pltpu.VMEM((NT, (H + 2) * WP, LANES), F32),
            pltpu.VMEM((NT, 16, LANES), F32),
            pltpu.VMEM((H * W, E), BF16),
            pltpu.VMEM((H // GROUP * SPLIT, depth, LANES), BF16),
            pltpu.VMEM((H // GROUP * SPLIT, depth, LANES), BF16),
            pltpu.VMEM((W // GROUP * SPLIT, depth, LANES), BF16),
            pltpu.VMEM((W // GROUP * SPLIT, depth, LANES), BF16),
            pltpu.VMEM((2, NT, W, LANES), BF16),
            pltpu.VMEM((2, NT, H, LANES), BF16),
            pltpu.VMEM((2, NT, W, LANES), BF16),
            pltpu.VMEM((6, NT, H, LANES), BF16),
            dma((2, 2)),
            dma((2, H // GROUP * SPLIT)),
            dma((2, W // GROUP * SPLIT)),
            dma((2, 8)),
            dma((2,)),
        ],
        compiler_params=pltpu.CompilerParams(
            collective_id=0, has_side_effects=True, vmem_limit_bytes=60 * 1024 * 1024
        ),
    )(
        features,
        gate_input,
        decay_idx,
        log_table,
        state_rate,
        proj_row.T,
        proj_col.T,
        conv_w,
        conv_b.reshape(1, E),
        d_skip.reshape(1, E),
    )


def solution(mesh):
    tile = P(("slides", "rows"), "cols", "chan")
    placed = (
        tile,
        tile,
        P(("slides", "rows"), "cols"),
        P(None, "chan"),
        P(),
        P("chan", None),
        P("chan", None),
        P(None, None, "chan"),
        P("chan"),
        P("chan"),
    )
    return jax.shard_map(
        functools.partial(shards, mesh.shape["rows"], mesh.shape["cols"]),
        mesh=mesh,
        in_specs=placed,
        out_specs=tile,
        check_vma=False,
    )
```

```python
import functools
import math

import jax
import jax.numpy as jnp
from jax import lax
from jax.experimental import pallas as pl
from jax.experimental.pallas import tpu as pltpu
from jax.sharding import PartitionSpec as P

MESH = pl.DeviceIdType.MESH
LANES = 128
GROUP = 8
PAD = 8
ROW_SPLIT = 2
COL_SPLIT = 4
ROW_UNROLL = 32
COL_UNROLL = 16
F32 = jnp.float32
BF16 = jnp.bfloat16
SIDES = ((-1, 0), (1, 0), (0, -1), (0, 1), (-1, -1), (-1, 1), (1, -1), (1, 1))


def opposite(side):
    return SIDES.index((-side[0], -side[1]))


def project(vals, proj_t):
    return lax.dot_general(vals, proj_t, (((1,), (1,)), ((), ())), preferred_element_type=F32)


def layer(
    dims,
    feats_hbm,
    gate_hbm,
    idx_ref,
    table_ref,
    rate_ref,
    proj_row_ref,
    proj_col_ref,
    conv_w_ref,
    conv_b_ref,
    skip_ref,
    out_ref,
    feats_ref,
    gate_ref,
    xf,
    yf,
    lf,
    hot,
    cf,
    csend,
    crecv,
    ro,
    par,
    mb,
    rsend,
    rrecv,
    zsend,
    zrecv,
    edge_rows,
    edge_cols,
    got_rows,
    got_cols,
    coeff_sems,
    row_sems,
    col_sems,
    edge_sems,
    load_sems,
):
    H, W, E, S, K, nz, nx = dims
    NT = -(-E // LANES)
    WP = W + 2 * PAD
    widths = [min(LANES, E - LANES * t) for t in range(NT)]
    z, x, c, sl = (lax.axis_index(a) for a in ("rows", "cols", "chan", "slides"))
    sibling = (sl, z, x, 1 - c)

    def exists(side):
        dz, dx = side
        parts = []
        if dz:
            parts.append(z > 0 if dz < 0 else z < nz - 1)
        if dx:
            parts.append(x > 0 if dx < 0 else x < nx - 1)
        return functools.reduce(jnp.logical_and, parts)

    def device(side):
        return (sl, z + side[0], x + side[1], c)

    feats_load = pltpu.make_async_copy(feats_hbm, feats_ref, load_sems.at[0])
    gate_load = pltpu.make_async_copy(gate_hbm, gate_ref, load_sems.at[1])
    feats_load.start()
    gate_load.start()
    barrier = pltpu.get_barrier_semaphore()
    pl.semaphore_signal(barrier, inc=1, device_id=sibling, device_id_type=MESH)
    for side in SIDES:

        @pl.when(exists(side))
        def _(side=side):
            pl.semaphore_signal(barrier, inc=1, device_id=device(side), device_id_type=MESH)

    feats_load.wait()
    flat = feats_ref[...].reshape(H * W, E)
    csend[0] = project(flat, proj_row_ref[...])
    peers_z = jnp.where(z > 0, 1, 0) + jnp.where(z < nz - 1, 1, 0)
    peers_x = jnp.where(x > 0, 1, 0) + jnp.where(x < nx - 1, 1, 0)
    pl.semaphore_wait(barrier, 1 + peers_z + peers_x + peers_z * peers_x)

    def coeff_copy(n):
        return pltpu.make_async_remote_copy(
            src_ref=csend.at[n],
            dst_ref=crecv.at[n],
            send_sem=coeff_sems.at[0, n],
            recv_sem=coeff_sems.at[1, n],
            device_id=sibling,
            device_id_type=MESH,
        )

    coeff_copy(0).start()

    for t in range(NT):
        w_t = widths[t]
        lo = t * LANES
        if w_t < LANES:
            xf[t] = jnp.zeros((H * W, LANES), F32)
            lf[t] = jnp.zeros((H * W, LANES), F32)
            par[t] = jnp.zeros((16, LANES), F32)
        xf[t, :, 0:w_t] = flat[:, lo : lo + w_t].astype(F32)
        for a in range(3):
            par[t, 3 * a : 3 * a + 3, 0:w_t] = conv_w_ref[a, :, lo : lo + w_t]
        par[t, 9:10, 0:w_t] = conv_b_ref[:, lo : lo + w_t]
        par[t, 10:11, 0:w_t] = skip_ref[:, lo : lo + w_t]
        ro[t] = jnp.zeros(((H + 2) * WP, LANES), F32)
    idx_t = idx_ref[...].astype(F32).T
    entry = lax.rem(lax.broadcasted_iota(jnp.int32, (W, 3 * K), 1), K).astype(F32)
    for h in range(H):
        hot[h * W : (h + 1) * W, :] = jnp.where(idx_t[:, h : h + 1] == entry, 1.0, 0.0)
    table = table_ref[...] * math.log2(math.e)
    first = table.astype(BF16)
    rest = table - first.astype(F32)
    second = rest.astype(BF16)
    third = (rest - second.astype(F32)).astype(BF16)
    logs = jnp.dot(
        hot[...].astype(BF16),
        jnp.concatenate([first, second, third], axis=0),
        preferred_element_type=F32,
    )
    for t in range(NT):
        lf[t, :, 0 : widths[t]] = logs[:, t * LANES : t * LANES + widths[t]]
    skips = [par[t, 10:11, :] for t in range(NT)]

    coeff_copy(0).wait()
    cf[:, 0 : 2 * S] = csend[0] + crecv[0]

    packed = widths[-1] <= LANES // 2
    low_lanes = lax.broadcasted_iota(jnp.int32, (GROUP, LANES), 1) < LANES // 2

    def scan_step(rows_at, q, sums, states):
        SQ = len(states) // NT
        coeffs = cf[rows_at, :]
        vals = [xf[t, rows_at, :] for t in range(NT)]
        logs_at = [lf[t, rows_at, :] for t in range(NT)]
        if q == 0:
            sums = [vals[t] * skips[t] for t in range(NT)]
        new = []
        for k in range(SQ):
            s = q * SQ + k
            b = jnp.broadcast_to(coeffs[:, s : s + 1], (GROUP, LANES))
            o = jnp.broadcast_to(coeffs[:, S + s : S + s + 1], (GROUP, LANES))
            for t in range(NT):
                state = jnp.exp2(logs_at[t] * rate_ref[s]) * states[k * NT + t] + b * vals[t]
                sums[t] = sums[t] + o * state
                new.append(state)
        return sums, tuple(new)

    def carry_copy(send, recv, sems, n, side):
        return pltpu.make_async_remote_copy(
            src_ref=send.at[n],
            dst_ref=recv.at[n],
            send_sem=sems.at[0, n],
            recv_sem=sems.at[1, n],
            device_id=device(side),
            device_id_type=MESH,
        )

    def half_turn(v):
        return pltpu.roll(v, LANES // 2, axis=1)

    def load_carry(recv, n, SQ):
        states = [None] * (SQ * NT)
        at = 0
        for t in range(NT):
            tail = packed and t == NT - 1
            for k in range(0, SQ, 4 if tail else 2):
                pair = recv[n, at : at + 2 * GROUP, :].astype(F32)
                at += 2 * GROUP
                for i in range(2):
                    v = pair[i * GROUP : (i + 1) * GROUP]
                    if tail:
                        states[(k + 2 * i) * NT + t] = jnp.where(low_lanes, v, 0.0)
                        states[(k + 2 * i + 1) * NT + t] = jnp.where(low_lanes, half_turn(v), 0.0)
                    else:
                        states[(k + i) * NT + t] = v
        return tuple(states)

    def store_carry(send, n, states):
        SQ = len(states) // NT
        at = 0
        for t in range(NT):
            tail = packed and t == NT - 1
            own = [states[k * NT + t] for k in range(SQ)]
            if tail:
                own = [own[k] + half_turn(own[k + 1]) for k in range(0, SQ, 2)]
            for k in range(0, len(own), 2):
                pair = jnp.concatenate([own[k], own[k + 1]], axis=0)
                send[n, at : at + 2 * GROUP, :] = pair.astype(BF16)
                at += 2 * GROUP

    @pl.when(x == 0)
    def _():
        rrecv[...] = jnp.zeros(rrecv.shape, BF16)

    for n in range(H // GROUP):
        for q in range(ROW_SPLIT):
            m = n * ROW_SPLIT + q

            @pl.when(x > 0)
            def _():
                carry_copy(rsend, rrecv, row_sems, m, (0, 1)).wait_recv()

            def row_step(w, states):
                to = pl.ds((n * GROUP + 1) * WP + PAD + w, GROUP, stride=WP)
                sums = [ro[t, to, :] for t in range(NT)] if q else None
                at = pl.ds(n * GROUP * W + w, GROUP, stride=W)
                sums, new = scan_step(at, q, sums, states)
                for t in range(NT):
                    last = q == ROW_SPLIT - 1
                    ro[t, to, :] = sums[t].astype(BF16).astype(F32) if last else sums[t]
                return new

            ends = lax.fori_loop(0, W, row_step, load_carry(rrecv, m, S // ROW_SPLIT), unroll=ROW_UNROLL)

            @pl.when(x < nx - 1)
            def _():
                store_carry(rsend, m, ends)
                carry_copy(rsend, rrecv, row_sems, m, (0, 1)).start()

    for t in range(NT):
        for n, h in enumerate((0, H - 1)):
            at = (h + 1) * WP + PAD
            edge_rows[n, t] = ro[t, at : at + W, :].astype(BF16)
        for n, w in enumerate((0, W - 1)):
            edge_cols[n, t] = ro[t, pl.ds(WP + PAD + w, H, stride=WP), :].astype(BF16)

    def edge_copy(k):
        dz, dx = SIDES[k]
        if dx == 0:
            src, dst = edge_rows.at[(dz + 1) // 2], got_rows.at[(1 - dz) // 2]
        else:
            src = edge_cols.at[(dx + 1) // 2]
            dst = got_cols.at[opposite(SIDES[k]) - 2]
        return pltpu.make_async_remote_copy(
            src_ref=src,
            dst_ref=dst,
            send_sem=edge_sems.at[0, k],
            recv_sem=edge_sems.at[1, opposite(SIDES[k])],
            device_id=device(SIDES[k]),
            device_id_type=MESH,
        )

    def edge_arrival(k):
        dz, dx = SIDES[k]
        buf = got_rows.at[(dz + 1) // 2] if dx == 0 else got_cols.at[k - 2]
        src = edge_rows.at[0] if dx == 0 else edge_cols.at[0]
        return pltpu.make_async_remote_copy(
            src_ref=src,
            dst_ref=buf,
            send_sem=edge_sems.at[0, k],
            recv_sem=edge_sems.at[1, k],
            device_id=device(SIDES[k]),
            device_id_type=MESH,
        )

    for k, side in enumerate(SIDES):

        @pl.when(exists(side))
        def _(k=k):
            edge_copy(k).start()

    def arrive(k, side):

        @pl.when(exists(side))
        def _():
            edge_arrival(k).wait_recv()
            dz, dx = side
            row = {-1: 0, 0: 1, 1: H + 1}[dz]
            col = {-1: PAD - 1, 0: PAD, 1: PAD + W}[dx]
            for t in range(NT):
                if dx == 0:
                    ro[t, row * WP + col : row * WP + col + W, :] = got_rows[
                        (dz + 1) // 2, t
                    ].astype(F32)
                elif dz == 0:
                    ro[t, pl.ds(row * WP + col, H, stride=WP), :] = got_cols[k - 2, t].astype(F32)
                else:
                    pick = H - 1 if dz < 0 else 0
                    ro[t, row * WP + col : row * WP + col + 1, :] = got_cols[k - 2, t].astype(F32)[
                        pick : pick + 1
                    ]

    def conv_step(h, unused):
        for t in range(NT):
            acc = jnp.broadcast_to(par[t, 9:10, :], (W, LANES))
            for a in range(3):
                for b in range(3):
                    start = (h + a) * WP
                    acc = acc + par[t, 3 * a + b : 3 * a + b + 1, :] * ro[
                        t, pl.ds(start + PAD - 1 + b, W), :
                    ]
            mid = (acc / (1.0 + jnp.exp(-acc))).astype(BF16)
            at = pl.ds(pl.multiple_of(h * W, W), W)
            xf[t, at, :] = mid.astype(F32)
            mb[at, t * LANES : t * LANES + widths[t]] = mid[:, 0 : widths[t]]
        return unused

    across = [k for k, side in enumerate(SIDES) if side[0] == 0]
    for k in across:
        arrive(k, SIDES[k])
    lax.fori_loop(1, H - 1, conv_step, 0, unroll=2 - H % 2)
    for k, side in enumerate(SIDES):
        if k not in across:
            arrive(k, side)
    for h in (0, H - 1):
        conv_step(h, 0)

    csend[1] = project(mb[...], proj_col_ref[...])
    coeff_copy(1).start()
    coeff_copy(1).wait()
    cf[:, 0 : 2 * S] = csend[1] + crecv[1]

    @pl.when(z == 0)
    def _():
        zrecv[...] = jnp.zeros(zrecv.shape, BF16)

    for n in range(W // GROUP):
        for q in range(COL_SPLIT):
            m = n * COL_SPLIT + q

            @pl.when(z > 0)
            def _():
                carry_copy(zsend, zrecv, col_sems, m, (1, 0)).wait_recv()

            def col_step(h, states):
                at = pl.ds(pl.multiple_of(h * W + n * GROUP, GROUP), GROUP)
                sums = [yf[t, at, :] for t in range(NT)] if q else None
                sums, new = scan_step(at, q, sums, states)
                for t in range(NT):
                    yf[t, at, :] = sums[t]
                return new

            ends = lax.fori_loop(0, H, col_step, load_carry(zrecv, m, S // COL_SPLIT), unroll=COL_UNROLL)

            @pl.when(z < nz - 1)
            def _():
                store_carry(zsend, m, ends)
                carry_copy(zsend, zrecv, col_sems, m, (1, 0)).start()

    gate_load.wait()
    def gate_step(h, unused):
        at = pl.ds(pl.multiple_of(h * W, W), W)
        for t in range(NT):
            g = gate_ref[h, :, t * LANES : t * LANES + widths[t]].astype(F32)
            v = yf[t, at, 0 : widths[t]] * g / (1.0 + jnp.exp(-g))
            out_ref[h, :, t * LANES : t * LANES + widths[t]] = v.astype(BF16)
        return unused

    lax.fori_loop(0, H, gate_step, 0, unroll=4)

    for k, side in enumerate(SIDES):

        @pl.when(exists(side))
        def _(k=k):
            edge_copy(k).wait_send()

    @pl.when(x < nx - 1)
    def _():
        for n in range(H // GROUP * ROW_SPLIT):
            carry_copy(rsend, rrecv, row_sems, n, (0, 1)).wait_send()

    @pl.when(z < nz - 1)
    def _():
        for n in range(W // GROUP * COL_SPLIT):
            carry_copy(zsend, zrecv, col_sems, n, (1, 0)).wait_send()


def shards(
    nz,
    nx,
    features,
    gate_input,
    decay_idx,
    log_table,
    state_rate,
    proj_row,
    proj_col,
    conv_w,
    conv_b,
    d_skip,
):
    H, W, E = features.shape
    S, K = state_rate.shape[0], log_table.shape[0]
    NT = -(-E // LANES)
    WP = W + 2 * PAD
    tail = E - (NT - 1) * LANES
    depth = (2 * NT - (tail <= LANES // 2)) * S * GROUP // 2
    vmem = pl.BlockSpec(memory_space=pltpu.VMEM)
    hbm = pl.BlockSpec(memory_space=pl.ANY)
    smem = pl.BlockSpec(memory_space=pltpu.SMEM)
    dma = pltpu.SemaphoreType.DMA
    return pl.pallas_call(
        functools.partial(layer, (H, W, E, S, K, nz, nx)),
        out_shape=jax.ShapeDtypeStruct((H, W, E), BF16),
        in_specs=[hbm] * 2 + [vmem] * 2 + [smem] + [vmem] * 5,
        out_specs=vmem,
        scratch_shapes=[
            pltpu.VMEM((H, W, E), BF16),
            pltpu.VMEM((H, W, E), BF16),
            pltpu.VMEM((NT, H * W, LANES), F32),
            pltpu.VMEM((NT, H * W, LANES), F32),
            pltpu.VMEM((NT, H * W, LANES), F32),
            pltpu.VMEM((H * W, 3 * K), F32),
            pltpu.VMEM((H * W, LANES), F32),
            pltpu.VMEM((2, H * W, 2 * S), F32),
            pltpu.VMEM((2, H * W, 2 * S), F32),
            pltpu.VMEM((NT, (H + 2) * WP, LANES), F32),
            pltpu.VMEM((NT, 16, LANES), F32),
            pltpu.VMEM((H * W, E), BF16),
            pltpu.VMEM((H // GROUP * ROW_SPLIT, depth // ROW_SPLIT, LANES), BF16),
            pltpu.VMEM((H // GROUP * ROW_SPLIT, depth // ROW_SPLIT, LANES), BF16),
            pltpu.VMEM((W // GROUP * COL_SPLIT, depth // COL_SPLIT, LANES), BF16),
            pltpu.VMEM((W // GROUP * COL_SPLIT, depth // COL_SPLIT, LANES), BF16),
            pltpu.VMEM((2, NT, W, LANES), BF16),
            pltpu.VMEM((2, NT, H, LANES), BF16),
            pltpu.VMEM((2, NT, W, LANES), BF16),
            pltpu.VMEM((6, NT, H, LANES), BF16),
            dma((2, 2)),
            dma((2, H // GROUP * ROW_SPLIT)),
            dma((2, W // GROUP * COL_SPLIT)),
            dma((2, 8)),
            dma((2,)),
        ],
        compiler_params=pltpu.CompilerParams(
            collective_id=0, has_side_effects=True, vmem_limit_bytes=60 * 1024 * 1024
        ),
    )(
        features,
        gate_input,
        decay_idx,
        log_table,
        state_rate,
        proj_row.T,
        proj_col.T,
        conv_w,
        conv_b.reshape(1, E),
        d_skip.reshape(1, E),
    )


def solution(mesh):
    tile = P(("slides", "rows"), "cols", "chan")
    placed = (
        tile,
        tile,
        P(("slides", "rows"), "cols"),
        P(None, "chan"),
        P(),
        P("chan", None),
        P("chan", None),
        P(None, None, "chan"),
        P("chan"),
        P("chan"),
    )
    return jax.shard_map(
        functools.partial(shards, mesh.shape["rows"], mesh.shape["cols"]),
        mesh=mesh,
        in_specs=placed,
        out_specs=tile,
        check_vma=False,
    )
```
